32 devices in a mesh: ctx: 8 (over z, core), exp: 4 (over y, x).
Axes of the slice: x: 2, y: 2, z: 4, core: 2. Of those that a mesh axis runs over, the one named last changes fastest.
Arguments:
- queries: bfloat16 [1024, 6144], P('ctx', 'exp'), may hold values from -12 to 12
- keys_values: bfloat16 [1024, 8, 256], P('ctx', 'exp'), may hold values from -12 to 12
- doc_ids: int32 [1024], P('ctx'), may hold values from 0 to 7, never falling along the last dimension, each value on 1 to 768 neighbouring positions
- gate_up: bfloat16 [4, 640, 16384], P('exp', None, 'ctx'), may hold values from -6 to 6
- down_weight: bfloat16 [4, 16384, 6144], P('exp', 'ctx'), may hold values from -0.046875 to 0.046875
- routes: int32 [1024, 2], P(('ctx', 'exp')), may hold values from 0 to 3, all different within a row; in each aligned block of 32 rows (0 to 31, 32 to 63, ...) at most 20 rows name the same one
- route_weights: float32 [1024, 2], P(('ctx', 'exp')), may hold values from 0.1 to 1
Outputs:
- context: bfloat16 [1024, 6144], P('ctx', 'exp')
- moe_out: bfloat16 [1024, 6144], P(('ctx', 'exp'))
The draws below stay inside these ranges and needn't reach their ends.
Inputs may be any that keep to these rules, and one draw needn't show every extreme that they name: doc_ids never falls along the sequence; each document has 1 to 768 tokens and one has exactly 768. `routes`: the 2 experts of a token differ; among the 32 tokens of one device (aligned blocks) no expert is named more than 20 times, a bound that some block reaches.
All inputs are finite; a program needn't handle non-finite values.
Results may differ from the reference program's by a relative error of at most 0.025.
Values may be sent and summed in bfloat16 or wider, within the bound.
A program may use at most 128 MiB of HBM per device.

```python
import math
import jax
import jax.numpy as jnp
import numpy as np
from jax import lax

D = 6144
FF = 16384
HQ = 48
KVH = 8
HD = 128
TOP = 2
DOCS = 8
EXPERTS = 4
SEQ = 1024
MOE_DEV = 32
CAP = 20
SLOTS = 640
FF_DEV = 2048
DOC_MOST = 768


def base_values(key, shape):
    return jax.random.truncated_normal(key, -5.0, 5.0, shape, jnp.float32)


def draw_keys_values(key, part):
    own = jax.random.fold_in(key, 11)
    key_keys, key_values = jax.random.split(own, 2)
    keys = base_values(key_keys, (SEQ, KVH, HD))
    values = base_values(key_values, (SEQ, KVH, HD))
    return jnp.concatenate([keys, values], axis=-1).astype(jnp.bfloat16)


def draw_queries(key, part):
    own = jax.random.fold_in(key, 13)
    queries = base_values(own, (SEQ, HQ, HD))
    return queries.reshape(SEQ, HQ * HD).astype(jnp.bfloat16)


def with_spikes(array, own_key, source, target, parts, factor):
    owner, partner = [(jnp.arange(array.shape[dim]) // (array.shape[dim] // parts)).reshape([-1 if axis == dim else 1 for axis in range(array.ndim)]) for dim in (source, target)]
    chosen = jax.random.permutation(own_key, parts)[partner]
    strong = (owner == chosen) | (owner == (partner + parts // 2) % parts)
    return jnp.where(strong, factor * array, array)


def levels(stream_key, dims, cuts, least, top_value):
    factor_of = 1.0
    for axis_at, parts in cuts:
        steps = jax.random.uniform(jax.random.fold_in(jax.random.fold_in(stream_key, 6), axis_at), (parts,), jnp.float32, least / len(cuts), top_value / len(cuts))
        factor_of = factor_of * jnp.repeat(jnp.exp(steps), dims[axis_at] // parts).reshape((-1,) + (1,) * (len(dims) - 1 - axis_at))
    return factor_of


def length_profile(count, total, most, skew):
    loads = [(1 << 20) // math.isqrt(rank ** skew) + 1 for rank in range(2, count + 1)]
    rest, holding = total - most - (count - 1), [1] * (count - 1)
    while rest > 0:
        candidates = [i for i in range(count - 1) if holding[i] < most]
        mass, budget = sum([loads[i] for i in candidates]), rest
        for i in candidates:
            more = min(most - holding[i], max(1, budget * loads[i] // mass), rest)
            holding[i] = holding[i] + more
            rest = rest - more
    return np.array([most] + holding)


def uneven(rng, number_of, total, bound, slope):
    if number_of == 2:
        one = jax.random.randint(rng, (), max(1, total - bound), min(bound, total - 1) + 1)
        return jnp.stack([one, total - one])
    sizes = jnp.asarray(length_profile(number_of, total, bound, slope), jnp.int32)
    pairs = (number_of - 1) // 2
    source_of, receiver = sizes[1:1 + 2 * pairs:2], sizes[2:2 + 2 * pairs:2]
    room = jnp.minimum(source_of - 1, bound - receiver)
    passed = jax.random.randint(jax.random.fold_in(rng, 1), (pairs,), 0, 1 << 20) % (room + 1)
    sizes = sizes.at[1:1 + 2 * pairs:2].set(source_of - passed).at[2:2 + 2 * pairs:2].set(receiver + passed)
    return sizes[jax.random.permutation(jax.random.fold_in(rng, 2), number_of)]


def deal_out(rng, own, number, rows, amount, top, bound, skew):
    order = jax.random.permutation(rng, amount)
    packed, usual = portions_of(amount, rows * top, bound, skew, True), portions_of(amount, rows * top, bound, skew, False)
    places = jnp.arange(amount)

    def named(tallies, rotation):
        used = int((tallies > 0).sum())
        fixed = max(1, used // 4)
        shifted = fixed + (places - fixed + rotation * (used - fixed)) % max(1, amount - fixed)
        return jnp.zeros((amount,), jnp.int32).at[order[jnp.where(places < fixed, places, shifted)]].set(jnp.asarray(tallies, jnp.int32))

    tallies = jnp.where(number % 4 == 0, named(packed, number // 4), named(usual, number - number // 4 - 1))
    mixed = jax.random.permutation(jax.random.fold_in(own, 3), amount)
    donor, receiver = mixed[0:amount // 2 * 2:2], mixed[1:amount // 2 * 2:2]
    room = jnp.minimum(tallies[donor] - 1, bound - tallies[receiver]) // 2
    room = jnp.where((donor == order[0]) | (receiver == order[0]) | (tallies[receiver] == 0), 0, jnp.maximum(room, 0))
    shifted = jax.random.randint(jax.random.fold_in(own, 4), (amount // 2,), 0, 1 << 20) % (room + 1)
    tallies = tallies.at[donor].add(-shifted).at[receiver].add(shifted)
    items = jnp.searchsorted(jnp.cumsum(tallies), jnp.arange(rows * top), side="right").astype(jnp.int32)
    grid = items.reshape(top, rows).T
    grid = grid[jax.random.permutation(jax.random.fold_in(own, 1), rows)]
    rotation = jax.random.randint(jax.random.fold_in(own, 2), (rows, 1), 0, top)
    return jnp.take_along_axis(grid, (jnp.arange(top)[None, :] + rotation) % top, axis=1)


def portions_of(amount, total, most, skew, full):
    loads = [(1 << 20) // math.isqrt(grade ** skew) + 1 for grade in range(1, amount + 1)]
    largest = most if full else min(most, max(-(-total // amount), total * loads[0] // sum(loads)))
    least = 1 if total - largest >= amount - 1 else 0
    holding, surplus = [largest] + [least] * (amount - 1), total - largest - least * (amount - 1)
    while surplus > 0:
        movable = [i for i in range(1, amount) if holding[i] < largest] or [i for i in range(1, amount) if holding[i] < most]
        pool, remaining = sum([loads[i] for i in movable]), surplus
        for i in movable:
            more = min(most - holding[i], max(1, remaining * loads[i] // pool), surplus)
            holding[i] = holding[i] + more
            surplus = surplus - more
    return np.array(holding)


def gaussian(own_key, dims, deviation, bound, cuts=(), kind=jnp.bfloat16):
    array = jax.random.normal(own_key, dims, jnp.float32) * deviation
    if len(cuts) > 0:
        array = levels(own_key, dims, cuts, -0.22, 0.18) * array
    return jnp.clip(array, min=-bound, max=bound).astype(kind)


def bell_draw_with(own_key, dims, deviation, most, pieces, heavy, kind=jnp.bfloat16):
    values = deviation * jax.random.normal(own_key, dims, jnp.float32)
    if pieces:
        values = values * levels(own_key, dims, pieces, -0.22, 0.18)
    return jnp.clip(with_spikes(values, jax.random.fold_in(own_key, 3), *heavy), -most, most).astype(kind)


def setup_inputs(seed: int = 0) -> dict:
    splits = jax.random.split(jax.random.key(seed), 8)
    queries = draw_queries(jax.random.fold_in(splits[7], 71), 0)
    keys_values = draw_keys_values(jax.random.fold_in(splits[7], 71), 0)
    doc_ids = jnp.searchsorted(jnp.cumsum(uneven(splits[2], DOCS, SEQ, DOC_MOST, 0)), jnp.arange(SEQ), side="right").astype(jnp.int32)
    gate_up = bell_draw_with(splits[3], (EXPERTS, SLOTS, FF), 1.0, 6.0, ((0, 4), (2, 8)), (2, 1, 8, 2.0))
    down_weight = gaussian(splits[4], (EXPERTS, FF, D), FF ** -0.5, 0.046875, ((0, 4), (1, 8)))
    routes_keys = jax.random.split(jax.random.fold_in(splits[5], 1), SEQ // MOE_DEV)
    routes_turns = jax.random.permutation(jax.random.fold_in(splits[5], 3), SEQ // MOE_DEV)
    routes = jax.vmap(lambda own, number: deal_out(jax.random.fold_in(splits[5], 2), own, number, MOE_DEV, EXPERTS, TOP, CAP, 2))(routes_keys, routes_turns).reshape((SEQ, TOP))
    route_weights = jnp.clip(jnp.exp(math.log(1.0) - 2.3025851 * jax.random.uniform(splits[6], (SEQ, TOP), jnp.float32) ** levels(splits[6], (SEQ, TOP), ((0, 32),), -0.2, 0.2)), 0.1, 1.0)
    return {"queries": queries, "keys_values": keys_values, "doc_ids": doc_ids, "gate_up": gate_up, "down_weight": down_weight, "routes": routes, "route_weights": route_weights}


def attention(queries, keys_values, doc_ids):
    groups = HQ // KVH
    blk = math.gcd(SEQ, 512)
    keys = keys_values[:, :, :HD].astype(jnp.float32)
    values = keys_values[:, :, HD:].astype(jnp.float32)
    positions = jnp.arange(SEQ, dtype=jnp.int32)
    scale = 1.0 / math.sqrt(HD)

    def attend(index):
        start = (index * blk).astype(jnp.int32)
        query_blk = lax.dynamic_slice_in_dim(queries, start, blk, 0).astype(jnp.float32).reshape(blk, KVH, groups, HD)
        doc_blk = lax.dynamic_slice_in_dim(doc_ids, start, blk, 0)
        pos_blk = start + jnp.arange(blk, dtype=jnp.int32)
        scores = jnp.einsum('qhgd,khd->hgqk', query_blk, keys) * scale
        allowed = (doc_blk[:, None] == doc_ids[None, :]) & (positions[None, :] <= pos_blk[:, None])
        scores = jnp.where(allowed, scores, jnp.float32(-1e+30))
        row_max = lax.optimization_barrier(jnp.max(scores, axis=-1, keepdims=True))
        weights = jnp.where(allowed, jnp.exp(scores - row_max), jnp.float32(0.0))
        denominator = lax.optimization_barrier(jnp.sum(weights, axis=-1))
        rounded = lax.optimization_barrier(weights.astype(jnp.bfloat16)).astype(jnp.float32)
        summed = jnp.einsum('hgqk,khd->qhgd', rounded, values)
        result = summed / jnp.transpose(denominator, (2, 0, 1))[..., None]
        return result.reshape(blk, HQ * HD).astype(jnp.bfloat16)
    blocks = lax.map(attend, jnp.arange(SEQ // blk, dtype=jnp.int32))
    return blocks.reshape(SEQ, HQ * HD)

def experts_out(gate_up, down_weight, routes, route_weights):
    spans = FF // FF_DEV

    def one_expert(expert):
        acts = gate_up[expert]
        weight = down_weight[expert]

        def step(total, span):
            start = (span * FF_DEV).astype(jnp.int32)
            acts_part = lax.dynamic_slice_in_dim(acts, start, FF_DEV, 1)
            weight_part = lax.dynamic_slice_in_dim(weight, start, FF_DEV, 0)
            part = jnp.dot(acts_part, weight_part, preferred_element_type=jnp.float32)
            part = lax.optimization_barrier(part.astype(jnp.bfloat16))
            return (total + part.astype(jnp.float32), None)
        total, _ = lax.scan(step, jnp.zeros((SLOTS, D), jnp.float32), jnp.arange(spans, dtype=jnp.int32))
        return total.astype(jnp.bfloat16)
    expert_rows = lax.map(one_expert, jnp.arange(EXPERTS, dtype=jnp.int32))
    flat = routes.reshape(SEQ // MOE_DEV, MOE_DEV * TOP)
    onehot = (flat[..., None] == jnp.arange(EXPERTS, dtype=jnp.int32)).astype(jnp.int32)
    earlier = jnp.cumsum(onehot, axis=1) - onehot
    slot = lax.optimization_barrier(jnp.sum(earlier * onehot, axis=-1)).reshape(SEQ, TOP)
    source = jnp.arange(SEQ, dtype=jnp.int32) // MOE_DEV
    row_index = source[:, None] * CAP + slot
    picked = expert_rows[routes, row_index].astype(jnp.float32)
    return lax.optimization_barrier(jnp.sum(route_weights[:, :, None] * picked, axis=1))

def reference(queries, keys_values, doc_ids, gate_up, down_weight, routes, route_weights):
    context = attention(queries, keys_values, doc_ids)
    mixed = experts_out(gate_up, down_weight, routes, route_weights)
    moe_out = (context.astype(jnp.float32) + mixed).astype(jnp.bfloat16)
    return (context, moe_out)
```

```python
import functools
import math

import jax
import jax.numpy as jnp
from jax import lax
from jax.experimental import pallas as pl
from jax.experimental.pallas import tpu as pltpu
from jax.sharding import PartitionSpec as P

MESH = pl.DeviceIdType.MESH
BF16 = jnp.bfloat16
F32 = jnp.float32
COLS = 512
WEIGHT_SLOTS = 4
DOC_ROWS = 16


def iota(shape, dim):
    return lax.broadcasted_iota(jnp.int32, shape, dim).astype(F32)


def whole_part(x, size):
    return jnp.floor((x + 0.5) * (1.0 / size))


def kernel(
    n_ctx, n_exp, steps,
    q_hbm, kv_ref, doc_ref, acts_hbm, w_hbm, routes_ref, rw_ref,
    ctx_ref, out_ref,
    q_buf, kv_buf, mask_buf, acts, acts_p, wbuf, csend, crecv, own, rows, mix_c, mix_w,
    zs, zr, fs, mixed, resid,
    in_sem, w_sem, c_ssem, c_rsem, x_ssem, x_rsem, z_ssem, z_rsem, f_ssem, f_rsem,
    k_ssem, k_rsem, p_ssem, p_rsem, m_ssem, m_rsem, r_ssem, r_rsem,
):
    ctx = lax.axis_index("ctx")
    exp = lax.axis_index("exp")
    core = lax.rem(ctx, 2)
    chip = lax.div(ctx, 2)
    mate = ctx + 1 - 2 * core
    n_chip = n_ctx // 2
    slots, depth = acts.shape
    group = slots // n_exp
    cap = group // n_ctx
    tok = routes_ref.shape[0]
    seq_rows = kv_ref.shape[0]
    half_cols = w_hbm.shape[2] // 2
    cols = COLS

    def w_copy(j):
        side = lax.rem(j + 1 + core, 2)
        start = pl.multiple_of(side * half_cols + lax.div(j, 2) * cols, 128)
        slot = lax.rem(j, WEIGHT_SLOTS)
        return pltpu.make_async_copy(
            w_hbm.at[0, :, pl.ds(start, cols)], wbuf.at[slot], w_sem.at[slot]
        )

    acts_copy = pltpu.make_async_copy(acts_hbm.at[0], acts, in_sem.at[0])
    q_copy = pltpu.make_async_copy(q_hbm, q_buf, in_sem.at[1])
    acts_copy.start()
    for j in range(WEIGHT_SLOTS):
        w_copy(jnp.int32(j)).start()
    q_copy.start()

    barrier = pltpu.get_barrier_semaphore()
    for d in range(1, n_ctx):
        pl.semaphore_signal(
            barrier, inc=1, device_id=(lax.rem(ctx + d, n_ctx), exp), device_id_type=MESH
        )
    for d in range(1, n_exp):
        pl.semaphore_signal(
            barrier, inc=1, device_id=(ctx, lax.rem(exp + d, n_exp)), device_id_type=MESH
        )

    kv_buf[ctx, 0:seq_rows, :] = kv_ref[...]
    doc_row = doc_ref[...].astype(F32)
    kv_buf[ctx, seq_rows:, 0:seq_rows] = jnp.broadcast_to(
        doc_row, (DOC_ROWS, seq_rows)
    ).astype(BF16)
    for i in range(n_chip):
        @pl.when(i > chip)
        def _():
            kv_buf[2 * i] = jnp.zeros(kv_buf.shape[1:], BF16)
            kv_buf[2 * i + 1] = jnp.zeros(kv_buf.shape[1:], BF16)

    wide = mix_c.shape[2]
    col = iota((tok, wide), 1)
    col_exp = whole_part(col, cap)
    col_slot = col - col_exp * cap
    is0 = routes_ref[:, 0:1].astype(F32) == col_exp
    is1 = routes_ref[:, 1:2].astype(F32) == col_exp
    named = jnp.where(is0 | is1, 1.0, 0.0).astype(BF16)
    before = jnp.where(iota((tok, tok), 1) < iota((tok, tok), 0), 1.0, 0.0).astype(BF16)
    earlier = jnp.dot(before, named, preferred_element_type=F32)
    gate = jnp.where(is0, rw_ref[:, 0:1], 0.0) + jnp.where(is1, rw_ref[:, 1:2], 0.0)
    mix_c[ctx] = jnp.where(earlier == col_slot, gate, 0.0).astype(BF16)

    def core_copy(s):
        return pltpu.make_async_remote_copy(
            csend.at[s], crecv.at[s], c_ssem.at[s], c_rsem.at[s],
            device_id=(mate, exp), device_id_type=MESH,
        )

    def rows_of(e):
        return pl.ds(pl.multiple_of(e * group, 16), group)

    def exp_copy(s, d, source=None):
        peer = lax.rem(exp + d, n_exp)
        source = exp if source is None else source
        return pltpu.make_async_remote_copy(
            crecv.at[s, rows_of(peer), :], rows.at[s, rows_of(source), :],
            x_ssem.at[s, d], x_rsem.at[s, source],
            device_id=(ctx, peer), device_id_type=MESH,
        )

    def z_copy(s, d, source=None):
        peer = lax.rem(chip + d, n_chip)
        source = chip if source is None else source
        return pltpu.make_async_remote_copy(
            zs.at[s, pl.ds(pl.multiple_of(peer * 2 * tok, 16), 2 * tok), :],
            zr.at[s, source], z_ssem.at[s, d], z_rsem.at[s, source],
            device_id=(2 * peer + core, exp), device_id_type=MESH,
        )

    def final_copy(s, side):
        return pltpu.make_async_remote_copy(
            fs.at[s], mixed.at[side, s], f_ssem.at[s], f_rsem.at[s],
            device_id=(mate, exp), device_id_type=MESH,
        )

    def kv_copy(d, source=None):
        source = chip if source is None else source
        block = kv_buf.at[2 * source + core]
        return pltpu.make_async_remote_copy(
            block, block, k_ssem.at[d], k_rsem.at[source],
            device_id=(lax.rem(ctx + 2 * d, n_ctx), exp), device_id_type=MESH,
        )

    def mate_copy(i, side):
        block = kv_buf.at[2 * i + side]
        return pltpu.make_async_remote_copy(
            block, block, p_ssem.at[i], p_rsem.at[i],
            device_id=(mate, exp), device_id_type=MESH,
        )

    def mix_copy(d, source=None):
        source = ctx if source is None else source
        return pltpu.make_async_remote_copy(
            mix_c.at[source], mix_c.at[source], m_ssem.at[d], m_rsem.at[source],
            device_id=(lax.rem(ctx + d, n_ctx), exp), device_id_type=MESH,
        )

    def resid_copy(d, source=None):
        peer = lax.rem(exp + d, n_exp)
        source = exp if source is None else source
        return pltpu.make_async_remote_copy(
            ctx_ref.at[pl.ds(pl.multiple_of(peer * tok, 16), tok), :], resid.at[source],
            r_ssem.at[d], r_rsem.at[source],
            device_id=(ctx, peer), device_id_type=MESH,
        )

    pl.semaphore_wait(barrier, n_ctx - 1 + n_exp - 1)
    mate_copy(chip, core).start()
    for d in range(1, n_chip):
        @pl.when(chip + d < n_chip)
        def _():
            kv_copy(d).start()
    for d in range(1, n_ctx):
        mix_copy(d).start()

    acts_copy.wait()
    place = iota((slots, 128), 0)
    place_exp = whole_part(place, group)
    place_rest = place - place_exp * group
    place_ctx = whole_part(place_rest, cap)
    came = (place_ctx * n_exp + place_exp) * cap + place_rest - place_ctx * cap
    order = jnp.where(iota((slots, slots), 1) == came[:, 0:1], 1.0, 0.0).astype(BF16)

    @pl.loop(0, depth // 512)
    def _(i):
        at = pl.ds(pl.multiple_of(i * 512, 128), 512)
        acts_p[:, at] = jnp.dot(order, acts[:, at], preferred_element_type=F32).astype(BF16)

    @pl.loop(0, steps)
    def _(s):
        for side in range(2):
            j = 2 * s + side
            w_copy(j).wait()
            product = jnp.dot(
                acts_p[...], wbuf[lax.rem(j, WEIGHT_SLOTS)], preferred_element_type=F32
            )
            if side == 0:
                csend[s] = product.astype(BF16)
                core_copy(s).start()
            else:
                own[...] = product

            @pl.when(j + WEIGHT_SLOTS < 2 * steps)
            def _():
                w_copy(j + WEIGHT_SLOTS).start()
        core_copy(s).wait_recv()
        crecv[s] = (own[...] + crecv[s].astype(F32)).astype(BF16)
        for d in range(1, n_exp):
            exp_copy(s, d).start()
        rows[s, rows_of(exp), :] = crecv[s, rows_of(exp), :]

    for d in range(1, n_ctx):
        mix_copy(d, lax.rem(ctx + d, n_ctx)).wait_recv()
    total_tok = n_ctx * tok
    at = iota((8, slots), 1)
    at_exp = whole_part(at, group)
    at_rest = at - at_exp * group
    at_ctx = whole_part(at_rest, cap)
    at_slot = at_exp * cap + at_rest - at_ctx * cap
    spread = jnp.where(iota((wide, slots), 0) == at_slot[0:1, :], 1.0, 0.0).astype(BF16)
    spread_w = jnp.dot(
        mix_c[...].reshape(total_tok, wide), spread, preferred_element_type=F32
    )
    token_ctx = whole_part(iota((total_tok, 128), 0), tok)[:, 0:1]
    mix_w[...] = jnp.where(token_ctx == at_ctx[0:1, :], spread_w, 0.0).astype(BF16)

    def combine(s):
        for d in range(1, n_exp):
            exp_copy(s, d, lax.rem(exp + d, n_exp)).wait_recv()
        zs[s] = jnp.dot(mix_w[...], rows[s], preferred_element_type=F32).astype(BF16)
        for d in range(1, n_chip):
            z_copy(s, d).start()

    def finish(s):
        for d in range(1, n_chip):
            z_copy(s, d, lax.rem(chip + d, n_chip)).wait_recv()

        def total_of(k):
            first = pl.multiple_of((2 * chip + k) * tok, 16)
            total = zs[s, pl.ds(first, tok), :].astype(F32)
            for d in range(1, n_chip):
                peer = lax.rem(chip + d, n_chip)
                part = zr[s, peer, pl.ds(pl.multiple_of(k * tok, 16), tok), :]
                total = total + part.astype(F32)
            return total.astype(BF16)

        fs[s] = total_of(1 - core)
        final_copy(s, core).start()
        mixed[core, s] = total_of(core)

    for i in range(n_chip - 1):
        @pl.when(i < chip)
        def _():
            kv_copy(1, i).wait_recv()
            mate_copy(i, core).start()
    combine(0)
    q_copy.wait()
    for i in range(n_chip):
        @pl.when(i <= chip)
        def _():
            mate_copy(i, 1 - core).wait_recv()

    seq = n_ctx * seq_rows
    key_doc = jnp.concatenate(
        [kv_buf[i, seq_rows:, 0:seq_rows].astype(F32)[0:1, :] for i in range(n_ctx)], axis=1
    )
    query_doc = jnp.broadcast_to(doc_row, (seq_rows, seq_rows)).T[:, 0:1]
    query_pos = lax.broadcasted_iota(jnp.int32, (seq_rows, seq), 0) + ctx * seq_rows
    key_pos = lax.broadcasted_iota(jnp.int32, (seq_rows, seq), 1)
    mask_buf[...] = jnp.where((query_doc == key_doc) & (key_pos <= query_pos), 0.0, -1e30)
    kv_heads = kv_ref.shape[1] // 256
    groups = q_buf.shape[1] // (kv_heads * 128)
    scale = 1.0 / math.sqrt(128)
    for g in range(kv_heads):
        @pl.loop(0, groups)
        def _(h):
            at = pl.ds(pl.multiple_of((g * groups + h) * 128, 128), 128)
            keys = kv_buf[:, 0:seq_rows, g * 256:g * 256 + 128].reshape(seq, 128)
            values = kv_buf[:, 0:seq_rows, g * 256 + 128:g * 256 + 256].reshape(seq, 128)
            scores = lax.dot_general(
                q_buf[:, at], keys, (((1,), (1,)), ((), ())), preferred_element_type=F32
            ) * scale + mask_buf[...]
            weights = jnp.exp(scores - jnp.max(scores, axis=1, keepdims=True))
            total = jnp.sum(weights, axis=1, keepdims=True)
            summed = jnp.dot(weights.astype(BF16), values, preferred_element_type=F32)
            ctx_ref[:, at] = (summed / total).astype(BF16)

    for d in range(1, n_exp):
        resid_copy(d).start()
    resid[exp] = ctx_ref[pl.ds(pl.multiple_of(exp * tok, 16), tok), :]

    @pl.loop(1, steps)
    def _(s):
        combine(s)
        finish(s - 1)

    finish(steps - 1)
    for d in range(1, n_exp):
        resid_copy(d, lax.rem(exp + d, n_exp)).wait_recv()
    for s in range(steps):
        final_copy(s, 1 - core).wait_recv()

    part = resid.shape[2]
    piece = math.gcd(cols, part)
    for first in range(0, 2 * half_cols, piece):
        side, rest = divmod(first, half_cols)
        s, off = divmod(rest, cols)
        e, inner = divmod(first, part)
        out_ref[:, first:first + piece] = (
            resid[e, :, inner:inner + piece].astype(F32)
            + mixed[side, s, :, off:off + piece].astype(F32)
        ).astype(BF16)

    @pl.loop(0, steps)
    def _(s):
        core_copy(s).wait_send()
        final_copy(s, core).wait_send()
        for d in range(1, n_exp):
            exp_copy(s, d).wait_send()
        for d in range(1, n_chip):
            z_copy(s, d).wait_send()

    for d in range(1, n_exp):
        resid_copy(d).wait_send()
    for d in range(1, n_ctx):
        mix_copy(d).wait_send()
    for i in range(n_chip):
        @pl.when(i <= chip)
        def _():
            mate_copy(i, core).wait_send()
    for d in range(1, n_chip):
        @pl.when(chip + d < n_chip)
        def _():
            kv_copy(d).wait_send()


def shards(n_ctx, n_exp, queries, keys_values, doc_ids, gate_up, down_weight, routes, route_weights):
    rows_q, width_q = queries.shape
    slots, depth = gate_up.shape[1:]
    width = down_weight.shape[2]
    tok = routes.shape[0]
    half = width // 2
    steps = half // COLS
    n_chip = n_ctx // 2
    cap = slots // (n_ctx * n_exp)
    wide = -(-n_exp * cap // 128) * 128
    kv = keys_values.reshape(rows_q, -1)
    dma = pltpu.SemaphoreType.DMA
    vmem = pl.BlockSpec(memory_space=pltpu.VMEM)
    hbm = pl.BlockSpec(memory_space=pl.ANY)
    return pl.pallas_call(
        functools.partial(kernel, n_ctx, n_exp, steps),
        out_shape=(
            jax.ShapeDtypeStruct((rows_q, width_q), BF16),
            jax.ShapeDtypeStruct((tok, width), BF16),
        ),
        in_specs=[hbm, vmem, vmem, hbm, hbm, vmem, vmem],
        out_specs=(vmem, vmem),
        scratch_shapes=[
            pltpu.VMEM((rows_q, width_q), BF16),
            pltpu.VMEM((n_ctx, rows_q + DOC_ROWS, kv.shape[1]), BF16),
            pltpu.VMEM((rows_q, n_ctx * rows_q), F32),
            pltpu.VMEM((slots, depth), BF16),
            pltpu.VMEM((slots, depth), BF16),
            pltpu.VMEM((WEIGHT_SLOTS, depth, COLS), BF16),
            pltpu.VMEM((steps, slots, COLS), BF16),
            pltpu.VMEM((steps, slots, COLS), BF16),
            pltpu.VMEM((slots, COLS), F32),
            pltpu.VMEM((steps, slots, COLS), BF16),
            pltpu.VMEM((n_ctx, tok, wide), BF16),
            pltpu.VMEM((n_ctx * tok, slots), BF16),
            pltpu.VMEM((steps, n_ctx * tok, COLS), BF16),
            pltpu.VMEM((steps, n_chip, 2 * tok, COLS), BF16),
            pltpu.VMEM((steps, tok, COLS), BF16),
            pltpu.VMEM((2, steps, tok, COLS), BF16),
            pltpu.VMEM((n_exp, tok, width_q), BF16),
            dma((2,)),
            dma((WEIGHT_SLOTS,)),
            dma((steps,)),
            dma((steps,)),
            dma((steps, n_exp)),
            dma((steps, n_exp)),
            dma((steps, n_chip)),
            dma((steps, n_chip)),
            dma((steps,)),
            dma((steps,)),
            dma((n_chip,)),
            dma((n_chip,)),
            dma((n_chip,)),
            dma((n_chip,)),
            dma((n_ctx,)),
            dma((n_ctx,)),
            dma((n_exp,)),
            dma((n_exp,)),
        ],
        compiler_params=pltpu.CompilerParams(
            collective_id=0, has_side_effects=True, vmem_limit_bytes=60 * 2**20
        ),
    )(queries, kv, doc_ids.reshape(1, -1), gate_up, down_weight, routes, route_weights)


def solution(mesh):
    in_specs = (
        P("ctx", "exp"),
        P("ctx", "exp", None),
        P("ctx"),
        P("exp", None, "ctx"),
        P("exp", "ctx", None),
        P(("ctx", "exp"), None),
        P(("ctx", "exp"), None),
    )
    out_specs = (P("ctx", "exp"), P(("ctx", "exp"), None))
    body = functools.partial(shards, mesh.shape["ctx"], mesh.shape["exp"])
    return jax.shard_map(body, mesh=mesh, in_specs=in_specs, out_specs=out_specs, check_vma=False)
```

```python
import functools
import math

import jax
import jax.numpy as jnp
from jax import lax
from jax.experimental import pallas as pl
from jax.experimental.pallas import tpu as pltpu
from jax.sharding import PartitionSpec as P

MESH = pl.DeviceIdType.MESH
BF16 = jnp.bfloat16
F32 = jnp.float32
COLS = 256
WEIGHT_SLOTS = 6
DOC_ROWS = 16


def iota(shape, dim):
    return lax.broadcasted_iota(jnp.int32, shape, dim).astype(F32)


def whole_part(x, size):
    return jnp.floor((x + 0.5) * (1.0 / size))


def kernel(
    n_ctx, n_exp, steps,
    q_hbm, kv_ref, doc_ref, acts_hbm, w_hbm, routes_ref, rw_ref,
    ctx_ref, out_ref,
    q_buf, kv_buf, mask_buf, acts, acts_p, wbuf, csend, crecv, own, rows, mix_c, mix_w,
    zs, zr, fs, mixed, resid,
    in_sem, w_sem, c_ssem, c_rsem, x_ssem, x_rsem, z_ssem, z_rsem, f_ssem, f_rsem,
    k_ssem, k_rsem, p_ssem, p_rsem, m_ssem, m_rsem, r_ssem, r_rsem,
):
    ctx = lax.axis_index("ctx")
    exp = lax.axis_index("exp")
    core = lax.rem(ctx, 2)
    chip = lax.div(ctx, 2)
    mate = ctx + 1 - 2 * core
    n_chip = n_ctx // 2
    slots, depth = acts.shape
    group = slots // n_exp
    cap = group // n_ctx
    tok = routes_ref.shape[1]
    seq_rows = kv_ref.shape[0]
    half_cols = w_hbm.shape[2] // 2
    cols = COLS

    def w_copy(j):
        side = lax.rem(j + 1 + core, 2)
        start = pl.multiple_of(side * half_cols + lax.div(j, 2) * cols, 128)
        slot = lax.rem(j, WEIGHT_SLOTS)
        return pltpu.make_async_copy(
            w_hbm.at[0, :, pl.ds(start, cols)], wbuf.at[slot], w_sem.at[slot]
        )

    acts_copy = pltpu.make_async_copy(acts_hbm.at[0], acts, in_sem.at[0])
    q_copy = pltpu.make_async_copy(q_hbm, q_buf, in_sem.at[1])
    acts_copy.start()
    for j in range(WEIGHT_SLOTS):
        w_copy(jnp.int32(j)).start()
    q_copy.start()

    barrier = pltpu.get_barrier_semaphore()
    for d in range(1, n_ctx):
        pl.semaphore_signal(
            barrier, inc=1, device_id=(lax.rem(ctx + d, n_ctx), exp), device_id_type=MESH
        )
    for d in range(1, n_exp):
        pl.semaphore_signal(
            barrier, inc=1, device_id=(ctx, lax.rem(exp + d, n_exp)), device_id_type=MESH
        )

    for g in range(kv_ref.shape[1]):
        kv_buf[ctx, 0:seq_rows, g * 256:(g + 1) * 256] = kv_ref[:, g, :]
    doc_row = doc_ref[...].astype(F32)
    kv_buf[ctx, seq_rows:, 0:seq_rows] = jnp.broadcast_to(
        doc_row, (DOC_ROWS, seq_rows)
    ).astype(BF16)
    for i in range(n_chip):
        @pl.when(i > chip)
        def _():
            kv_buf[2 * i] = jnp.zeros(kv_buf.shape[1:], BF16)
            kv_buf[2 * i + 1] = jnp.zeros(kv_buf.shape[1:], BF16)

    wide = mix_c.shape[2]
    col = iota((tok, wide), 1)
    col_exp = whole_part(col, cap)
    col_slot = col - col_exp * cap

    def upright(row):
        same = iota((tok, tok), 0) == iota((tok, tok), 1)
        return jnp.sum(jnp.where(same, row, 0.0), axis=1, keepdims=True)

    is0 = upright(routes_ref[0:1, :].astype(F32)) == col_exp
    is1 = upright(routes_ref[1:2, :].astype(F32)) == col_exp
    named = jnp.where(is0 | is1, 1.0, 0.0).astype(BF16)
    before = jnp.where(iota((tok, tok), 1) < iota((tok, tok), 0), 1.0, 0.0).astype(BF16)
    earlier = jnp.dot(before, named, preferred_element_type=F32)
    gate = jnp.where(is0, upright(rw_ref[0:1, :]), 0.0) + jnp.where(
        is1, upright(rw_ref[1:2, :]), 0.0
    )
    mix_c[ctx] = jnp.where(earlier == col_slot, gate, 0.0).astype(BF16)

    def core_copy(s):
        return pltpu.make_async_remote_copy(
            csend.at[s], crecv.at[s], c_ssem.at[s], c_rsem.at[s],
            device_id=(mate, exp), device_id_type=MESH,
        )

    def rows_of(e):
        return pl.ds(pl.multiple_of(e * group, 16), group)

    def exp_copy(s, d, source=None):
        peer = lax.rem(exp + d, n_exp)
        source = exp if source is None else source
        return pltpu.make_async_remote_copy(
            crecv.at[s, rows_of(peer), :], rows.at[s, rows_of(source), :],
            x_ssem.at[s, d], x_rsem.at[s, source],
            device_id=(ctx, peer), device_id_type=MESH,
        )

    def z_copy(s, d, source=None):
        peer = lax.rem(chip + d, n_chip)
        source = chip if source is None else source
        return pltpu.make_async_remote_copy(
            zs.at[s, pl.ds(pl.multiple_of(peer * 2 * tok, 16), 2 * tok), :],
            zr.at[s, source], z_ssem.at[s, d], z_rsem.at[s, source],
            device_id=(2 * peer + core, exp), device_id_type=MESH,
        )

    def final_copy(s, side):
        return pltpu.make_async_remote_copy(
            fs.at[s], mixed.at[side, s], f_ssem.at[s], f_rsem.at[s],
            device_id=(mate, exp), device_id_type=MESH,
        )

    def kv_copy(d, source=None):
        source = chip if source is None else source
        block = kv_buf.at[2 * source + core]
        return pltpu.make_async_remote_copy(
            block, block, k_ssem.at[d], k_rsem.at[source],
            device_id=(lax.rem(ctx + 2 * d, n_ctx), exp), device_id_type=MESH,
        )

    def mate_copy(i, side):
        block = kv_buf.at[2 * i + side]
        return pltpu.make_async_remote_copy(
            block, block, p_ssem.at[i], p_rsem.at[i],
            device_id=(mate, exp), device_id_type=MESH,
        )

    def mix_copy(d, source=None):
        source = ctx if source is None else source
        return pltpu.make_async_remote_copy(
            mix_c.at[source], mix_c.at[source], m_ssem.at[d], m_rsem.at[source],
            device_id=(lax.rem(ctx + d, n_ctx), exp), device_id_type=MESH,
        )

    def resid_copy(d, source=None):
        peer = lax.rem(exp + d, n_exp)
        source = exp if source is None else source
        return pltpu.make_async_remote_copy(
            ctx_ref.at[pl.ds(pl.multiple_of(peer * tok, 16), tok), :], resid.at[source],
            r_ssem.at[d], r_rsem.at[source],
            device_id=(ctx, peer), device_id_type=MESH,
        )

    pl.semaphore_wait(barrier, n_ctx - 1 + n_exp - 1)
    mate_copy(chip, core).start()
    for d in range(1, n_chip):
        @pl.when(chip + d < n_chip)
        def _():
            kv_copy(d).start()
    for d in range(1, n_ctx):
        mix_copy(d).start()

    acts_copy.wait()
    place = iota((slots, 128), 0)
    place_exp = whole_part(place, group)
    place_rest = place - place_exp * group
    place_ctx = whole_part(place_rest, cap)
    came = (place_ctx * n_exp + place_exp) * cap + place_rest - place_ctx * cap
    order = jnp.where(iota((slots, slots), 1) == came[:, 0:1], 1.0, 0.0).astype(BF16)

    @pl.loop(0, depth // 512)
    def _(i):
        at = pl.ds(pl.multiple_of(i * 512, 128), 512)
        acts_p[:, at] = jnp.dot(order, acts[:, at], preferred_element_type=F32).astype(BF16)

    def prepare():
        for d in range(1, n_ctx):
            mix_copy(d, lax.rem(ctx + d, n_ctx)).wait_recv()
        total_tok = n_ctx * tok
        at = iota((8, slots), 1)
        at_exp = whole_part(at, group)
        at_rest = at - at_exp * group
        at_ctx = whole_part(at_rest, cap)
        at_slot = at_exp * cap + at_rest - at_ctx * cap
        spread = jnp.where(iota((wide, slots), 0) == at_slot[0:1, :], 1.0, 0.0).astype(BF16)
        spread_w = jnp.dot(
            mix_c[...].reshape(total_tok, wide), spread, preferred_element_type=F32
        )
        token_ctx = whole_part(iota((total_tok, 128), 0), tok)[:, 0:1]
        mix_w[...] = jnp.where(token_ctx == at_ctx[0:1, :], spread_w, 0.0).astype(BF16)

    def combine(s):
        for d in range(1, n_exp):
            exp_copy(s, d, lax.rem(exp + d, n_exp)).wait_recv()
        zs[s] = jnp.dot(mix_w[...], rows[s], preferred_element_type=F32).astype(BF16)
        for d in range(1, n_chip):
            z_copy(s, d).start()

    @pl.loop(0, steps)
    def _(s):
        for side in range(2):
            j = 2 * s + side
            w_copy(j).wait()
            product = jnp.dot(
                acts_p[...], wbuf[lax.rem(j, WEIGHT_SLOTS)], preferred_element_type=F32
            )
            if side == 0:
                csend[s] = product.astype(BF16)
                core_copy(s).start()
            else:
                own[...] = product

            @pl.when(j + WEIGHT_SLOTS < 2 * steps)
            def _():
                w_copy(j + WEIGHT_SLOTS).start()
        core_copy(s).wait_recv()
        crecv[s] = (own[...] + crecv[s].astype(F32)).astype(BF16)
        for d in range(1, n_exp):
            exp_copy(s, d).start()
        rows[s, rows_of(exp), :] = crecv[s, rows_of(exp), :]

        @pl.when(s == 2)
        def _():
            prepare()

        @pl.when((s >= 3) & (lax.rem(s, 3) != 1))
        def _():
            combine(lax.div(2 * s, 3) - 2)

    def finish(s):
        for d in range(1, n_chip):
            z_copy(s, d, lax.rem(chip + d, n_chip)).wait_recv()

        def total_of(k):
            first = pl.multiple_of((2 * chip + k) * tok, 16)
            total = zs[s, pl.ds(first, tok), :].astype(F32)
            for d in range(1, n_chip):
                peer = lax.rem(chip + d, n_chip)
                part = zr[s, peer, pl.ds(pl.multiple_of(k * tok, 16), tok), :]
                total = total + part.astype(F32)
            return total.astype(BF16)

        fs[s] = total_of(1 - core)
        final_copy(s, core).start()
        mixed[core, s] = total_of(core)

    for i in range(n_chip - 1):
        @pl.when(i < chip)
        def _():
            kv_copy(1, i).wait_recv()
            mate_copy(i, core).start()
    q_copy.wait()
    for i in range(n_chip):
        @pl.when(i <= chip)
        def _():
            mate_copy(i, 1 - core).wait_recv()

    seq = n_ctx * seq_rows
    key_doc = jnp.concatenate(
        [kv_buf[i, seq_rows:, 0:seq_rows].astype(F32)[0:1, :] for i in range(n_ctx)], axis=1
    )
    query_doc = jnp.broadcast_to(doc_row, (seq_rows, seq_rows)).T[:, 0:1]
    query_pos = lax.broadcasted_iota(jnp.int32, (seq_rows, seq), 0) + ctx * seq_rows
    key_pos = lax.broadcasted_iota(jnp.int32, (seq_rows, seq), 1)
    mask_buf[...] = jnp.where((query_doc == key_doc) & (key_pos <= query_pos), 0.0, -1e30)
    kv_heads = kv_ref.shape[1]
    groups = q_buf.shape[1] // (kv_heads * 128)
    scale = 1.0 / math.sqrt(128)
    done = 2 * (steps - 1) // 3 - 1
    for g in range(kv_heads):
        @pl.loop(0, groups)
        def _(h):
            at = pl.ds(pl.multiple_of((g * groups + h) * 128, 128), 128)
            keys = kv_buf[:, 0:seq_rows, g * 256:g * 256 + 128].reshape(seq, 128)
            values = kv_buf[:, 0:seq_rows, g * 256 + 128:g * 256 + 256].reshape(seq, 128)
            scores = lax.dot_general(
                q_buf[:, at], keys, (((1,), (1,)), ((), ())), preferred_element_type=F32
            ) * scale + mask_buf[...]
            weights = jnp.exp(scores - jnp.max(scores, axis=1, keepdims=True))
            total = jnp.sum(weights, axis=1, keepdims=True)
            summed = jnp.dot(weights.astype(BF16), values, preferred_element_type=F32)
            ctx_ref[:, at] = (summed / total).astype(BF16)

        if g == 0:
            @pl.loop(done, done + 2)
            def _(s):
                combine(s)

    for d in range(1, n_exp):
        resid_copy(d).start()
    resid[exp] = ctx_ref[pl.ds(pl.multiple_of(exp * tok, 16), tok), :]

    @pl.loop(done + 2, steps)
    def _(s):
        combine(s)
        finish(s - done - 2)

    @pl.loop(steps - done - 2, steps)
    def _(s):
        finish(s)

    for d in range(1, n_exp):
        resid_copy(d, lax.rem(exp + d, n_exp)).wait_recv()
    for s in range(steps):
        final_copy(s, 1 - core).wait_recv()

    part = resid.shape[2]
    piece = math.gcd(cols, part)
    for first in range(0, 2 * half_cols, piece):
        side, rest = divmod(first, half_cols)
        s, off = divmod(rest, cols)
        e, inner = divmod(first, part)
        out_ref[:, first:first + piece] = (
            resid[e, :, inner:inner + piece].astype(F32)
            + mixed[side, s, :, off:off + piece].astype(F32)
        ).astype(BF16)

    @pl.loop(0, steps)
    def _(s):
        core_copy(s).wait_send()
        final_copy(s, core).wait_send()
        for d in range(1, n_exp):
            exp_copy(s, d).wait_send()
        for d in range(1, n_chip):
            z_copy(s, d).wait_send()

    for d in range(1, n_exp):
        resid_copy(d).wait_send()
    for d in range(1, n_ctx):
        mix_copy(d).wait_send()
    for i in range(n_chip):
        @pl.when(i <= chip)
        def _():
            mate_copy(i, core).wait_send()
    for d in range(1, n_chip):
        @pl.when(chip + d < n_chip)
        def _():
            kv_copy(d).wait_send()


def place_results(ctx_in, out_in, ctx_out, out_out, sem):
    first = pltpu.make_async_copy(ctx_in, ctx_out, sem.at[0])
    second = pltpu.make_async_copy(out_in, out_out, sem.at[1])
    first.start()
    second.start()
    first.wait()
    second.wait()


def shards(n_ctx, n_exp, queries, keys_values, doc_ids, gate_up, down_weight, routes, route_weights):
    rows_q, width_q = queries.shape
    slots, depth = gate_up.shape[1:]
    width = down_weight.shape[2]
    tok = routes.shape[0]
    half = width // 2
    steps = half // COLS
    n_chip = n_ctx // 2
    cap = slots // (n_ctx * n_exp)
    wide = -(-n_exp * cap // 128) * 128
    kv_width = keys_values.shape[1] * keys_values.shape[2]
    dma = pltpu.SemaphoreType.DMA
    vmem = pl.BlockSpec(memory_space=pltpu.VMEM)
    hbm = pl.BlockSpec(memory_space=pl.ANY)
    results = pl.pallas_call(
        functools.partial(kernel, n_ctx, n_exp, steps),
        out_shape=(
            jax.ShapeDtypeStruct((rows_q, width_q), BF16),
            jax.ShapeDtypeStruct((tok, width), BF16),
        ),
        in_specs=[hbm, vmem, vmem, hbm, hbm, vmem, vmem],
        out_specs=(vmem, vmem),
        scratch_shapes=[
            pltpu.VMEM((rows_q, width_q), BF16),
            pltpu.VMEM((n_ctx, rows_q + DOC_ROWS, kv_width), BF16),
            pltpu.VMEM((rows_q, n_ctx * rows_q), F32),
            pltpu.VMEM((slots, depth), BF16),
            pltpu.VMEM((slots, depth), BF16),
            pltpu.VMEM((WEIGHT_SLOTS, depth, COLS), BF16),
            pltpu.VMEM((steps, slots, COLS), BF16),
            pltpu.VMEM((steps, slots, COLS), BF16),
            pltpu.VMEM((slots, COLS), F32),
            pltpu.VMEM((steps, slots, COLS), BF16),
            pltpu.VMEM((n_ctx, tok, wide), BF16),
            pltpu.VMEM((n_ctx * tok, slots), BF16),
            pltpu.VMEM((steps, n_ctx * tok, COLS), BF16),
            pltpu.VMEM((steps, n_chip, 2 * tok, COLS), BF16),
            pltpu.VMEM((steps, tok, COLS), BF16),
            pltpu.VMEM((2, steps, tok, COLS), BF16),
            pltpu.VMEM((n_exp, tok, width_q), BF16),
            dma((2,)),
            dma((WEIGHT_SLOTS,)),
            dma((steps,)),
            dma((steps,)),
            dma((steps, n_exp)),
            dma((steps, n_exp)),
            dma((steps, n_chip)),
            dma((steps, n_chip)),
            dma((steps,)),
            dma((steps,)),
            dma((n_chip,)),
            dma((n_chip,)),
            dma((n_chip,)),
            dma((n_chip,)),
            dma((n_ctx,)),
            dma((n_ctx,)),
            dma((n_exp,)),
            dma((n_exp,)),
        ],
        compiler_params=pltpu.CompilerParams(
            collective_id=0, has_side_effects=True, vmem_limit_bytes=60 * 2**20
        ),
    )(
        queries, keys_values, doc_ids.reshape(1, -1), gate_up, down_weight,
        routes.T, route_weights.T,
    )
    return pl.pallas_call(
        place_results,
        out_shape=tuple(jax.ShapeDtypeStruct(r.shape, r.dtype) for r in results),
        in_specs=[hbm, hbm],
        out_specs=(hbm, hbm),
        scratch_shapes=[dma((2,))],
    )(*results)


def solution(mesh):
    in_specs = (
        P("ctx", "exp"),
        P("ctx", "exp", None),
        P("ctx"),
        P("exp", None, "ctx"),
        P("exp", "ctx", None),
        P(("ctx", "exp"), None),
        P(("ctx", "exp"), None),
    )
    out_specs = (P("ctx", "exp"), P(("ctx", "exp"), None))
    body = functools.partial(shards, mesh.shape["ctx"], mesh.shape["exp"])
    return jax.shard_map(body, mesh=mesh, in_specs=in_specs, out_specs=out_specs, check_vma=False)
```
